1024 devices in a mesh: occ: 8 (over x, core), vir: 128 (over y, z).
Axes of the slice: x: 4, y: 4, z: 32, core: 2. Of those that a mesh axis runs over, the one named last changes fastest.
Arguments:
- amps: bfloat16 [2048, 65536], P('occ', 'vir'), may hold values from -6 to 6
- integrals: bfloat16 [128, 5, 512, 512], P('vir'), may hold values from -0.25 to 0.25
- mask: int32 [128, 5], P('vir'), may hold values 0 or 1
- pair_coupling: bfloat16 [2048, 2048], P('occ'), may hold values from -0.125 to 0.125
- occ_energy: float32 [2048], P('occ'), may hold values from -2 to -0.5
- vir_energy: float32 [65536], P('vir'), may hold values from 0.5 to 4
Outputs:
- update: float32 [2048, 65536], P('occ', 'vir')
The draws below stay inside these ranges and needn't reach their ends.
All inputs are finite; a program needn't handle non-finite values. No bound on the sum of `mask` on one device may be relied on, other than what follows from the above.
Results may differ from the reference program's by a relative error of at most 0.0003.
Values may be sent and summed in bfloat16 or wider, within the bound.
No kernel may reach another device: no remote copies, remote signals or barrier semaphores. Data moves between devices by JAX's collectives and lax.ppermute only.
A program may use at most 32 MiB of HBM per device.

```python
import jax
import jax.numpy as jnp
from jax import lax

TILE = 512
REACH = 2
BLOCKS = 5
NTILES = 128
NVIR = 65536
OPAIRS = 2048


def place_ends(result, key, least, top_value):
    spot = [jax.random.randint(jax.random.fold_in(key, axis), (), 0, length) for axis, length in enumerate(result.shape)]
    main_axis = result.shape.index(max(result.shape))
    next_to = spot[:main_axis] + [(spot[main_axis] + 1) % result.shape[main_axis]] + spot[main_axis + 1:]
    return result.at[tuple(spot)].set(least).at[tuple(next_to)].set(top_value)


def steps_of(own_key, shape, shards, low, top_value):
    loudness, own = 1.0, jax.random.fold_in(own_key, 6)
    for dim, blocks in shards:
        draws = jnp.exp(jax.random.uniform(jax.random.fold_in(own, dim), (blocks,), jnp.float32, low / len(shards), top_value / len(shards)))
        loudness = loudness * jnp.repeat(draws, shape[dim] // blocks).reshape([-1 if axis == dim else 1 for axis in range(len(shape))])
    return loudness


def centred(rng, extent, width, limit, shards=(), kind=jnp.bfloat16):
    entries = jax.random.normal(rng, extent, jnp.float32) * width
    if len(shards) > 0:
        entries = steps_of(rng, extent, shards, -0.22, 0.18) * entries
    return jnp.clip(entries, min=-limit, max=limit).astype(kind)


def setup_inputs(seed: int = 0) -> dict:
    key_list = jax.random.split(jax.random.key(seed), 7)
    amps = centred(key_list[0], (OPAIRS, NVIR), 1.0, 6.0, ((0, 8), (1, 128)))
    integrals = centred(key_list[1], (NTILES, BLOCKS, TILE, TILE), TILE ** -0.5, 0.25, ((0, 128),))
    mask = place_ends((jax.random.randint(key_list[2], (NTILES, BLOCKS), 0, 3) < 2).astype(jnp.int32), jax.random.fold_in(key_list[2], 1), 0, 1)
    pair_coupling = centred(key_list[3], (OPAIRS, OPAIRS), OPAIRS ** -0.5, 0.125, ((0, 8),))
    occ_energy = jnp.clip(-2.0 + 1.5 * jax.random.uniform(key_list[4], (OPAIRS,), jnp.float32) ** steps_of(key_list[4], (OPAIRS,), ((0, 8),), -0.2, 0.2), -2.0, -0.5)
    vir_energy = jnp.clip(0.5 + 3.5 * jax.random.uniform(key_list[5], (NVIR,), jnp.float32) ** steps_of(key_list[5], (NVIR,), ((0, 128),), -0.2, 0.2), 0.5, 4.0)
    return {"amps": amps, "integrals": integrals, "mask": mask, "pair_coupling": pair_coupling, "occ_energy": occ_energy, "vir_energy": vir_energy}


def reference(amps, integrals, mask, pair_coupling, occ_energy, vir_energy):
    def one_tile(v):
        total = jnp.zeros((OPAIRS, TILE), jnp.float32)
        for k in range(BLOCKS):
            q = v - REACH + k
            inside = jnp.logical_and(q >= 0, q < NTILES)
            qc = jnp.clip(q, 0, NTILES - 1).astype(jnp.int32)
            left = lax.dynamic_slice_in_dim(amps, qc * TILE, TILE, 1)
            block = integrals[qc, k]
            flag = jnp.logical_and(inside, mask[qc, k] > 0)
            term = jnp.dot(left, block, preferred_element_type=jnp.float32)
            total = total + jnp.where(flag, term, jnp.zeros_like(term))
        own = lax.dynamic_slice_in_dim(amps, v.astype(jnp.int32) * TILE, TILE, 1)
        total = total + jnp.dot(pair_coupling, own, preferred_element_type=jnp.float32)
        energies = lax.dynamic_slice_in_dim(vir_energy, v.astype(jnp.int32) * TILE, TILE, 0)
        return total / (occ_energy[:, None] - energies[None, :])

    tiles = lax.map(one_tile, jnp.arange(NTILES, dtype=jnp.int32))
    return jnp.transpose(tiles, (1, 0, 2)).reshape(OPAIRS, NVIR)
```

```python
import jax
import jax.numpy as jnp
from jax import lax
from jax.sharding import PartitionSpec as P


def shifted(block, axis, distance):
    devices = range(lax.axis_size(axis))
    route = [(i - distance, i) for i in devices if i - distance in devices]
    return lax.ppermute(block, axis, route)


def body(amps, integrals, mask, pair_coupling, occ_energy, vir_energy):
    n = lax.axis_size("occ")
    scale = 64.0

    def term(k, left, factor=1.0):
        product = jnp.dot(left, integrals[0, k], preferred_element_type=jnp.float32)
        return product * (mask[0, k].astype(jnp.float32) * factor)

    right2 = term(0, amps, scale).astype(jnp.float16)
    right1 = term(1, amps, scale).astype(jnp.float16)
    far_r2, far_r1 = shifted(right2, "vir", 2), shifted(right1, "vir", 1)
    amps_g, right1_ = lax.optimization_barrier((amps, right1))
    wide = jnp.broadcast_to(amps_g[None], (n, *amps.shape))
    gathered = lax.all_to_all(wide, "occ", 0, 0).reshape(n * amps.shape[0], amps.shape[1])
    amps_l, _ = lax.optimization_barrier((amps_g, wide))
    left2 = term(4, amps_l, scale).astype(jnp.float16)
    left1 = term(3, amps_l, scale).astype(jnp.float16)
    far_l2, far_l1 = shifted(left2, "vir", -2), shifted(left1, "vir", -1)
    own = term(2, amps) + jnp.dot(pair_coupling, gathered, preferred_element_type=jnp.float32)
    far = (far_l2.astype(jnp.float32) + far_l1.astype(jnp.float32)) + (far_r2.astype(jnp.float32) + far_r1.astype(jnp.float32))
    total = own + far * (1.0 / scale)
    return total / (occ_energy[:, None] - vir_energy[None, :])


def solution(mesh):
    placed = (
        P("occ", "vir"),
        P("vir", None, None, None),
        P("vir", None),
        P("occ", None),
        P("occ"),
        P("vir"),
    )
    return jax.shard_map(
        body, mesh=mesh, in_specs=placed, out_specs=P("occ", "vir"), check_vma=False
    )
```

```python
import jax
import jax.numpy as jnp
from jax import lax
from jax.experimental import pallas as pl
from jax.experimental.pallas import tpu as pltpu
from jax.sharding import PartitionSpec as P

SCALE = 64.0
SENT = (1, 0, 3, 4)
CORES = 2
STEPS = (0, 2, 6, 4)
LIMIT = 8 * 2**20


def shifted(block, axis, distance):
    devices = range(lax.axis_size(axis))
    route = [(i - distance, i) for i in devices if i - distance in devices]
    return lax.ppermute(block, axis, route)


def terms_kernel(mask_ref, amps_ref, blocks_ref, *rest):
    out_refs, (held, sems) = rest[:4], rest[4:]
    loads = [
        pltpu.make_async_copy(blocks_ref.at[0, k], held.at[i], sems.at[i])
        for i, k in enumerate(SENT)
    ]
    for load in loads:
        load.start()
    for i, k in enumerate(SENT):
        loads[i].wait()
        flag = mask_ref[0, k].astype(jnp.float32) * SCALE
        out_refs[i][...] = flag * jnp.dot(
            amps_ref[...], held[i], preferred_element_type=jnp.float32
        )


def terms(mask, amps, integrals):
    rows, tile = amps.shape
    whole = pl.BlockSpec(memory_space=pltpu.VMEM)
    return pl.pallas_call(
        terms_kernel,
        out_shape=(jax.ShapeDtypeStruct((rows, tile), jnp.float32),) * 4,
        in_specs=[pl.BlockSpec(memory_space=pltpu.SMEM), whole, pl.BlockSpec(memory_space=pl.ANY)],
        out_specs=(whole,) * 4,
        scratch_shapes=[pltpu.VMEM((4, tile, tile), amps.dtype), pltpu.SemaphoreType.DMA((4,))],
        compiler_params=pltpu.CompilerParams(vmem_limit_bytes=LIMIT),
        cost_estimate=pl.CostEstimate(
            flops=8 * rows * tile * tile, bytes_accessed=8 * tile * tile, transcendentals=0
        ),
    )(mask, amps, integrals)


def join_kernel(*refs):
    for i, ref in enumerate(refs[:-1]):
        refs[-1][i] = ref[...]


def joined(parts):
    whole = pl.BlockSpec(memory_space=pltpu.VMEM)
    return pl.pallas_call(
        join_kernel,
        out_shape=jax.ShapeDtypeStruct((len(parts), *parts[0].shape), parts[0].dtype),
        in_specs=[whole] * len(parts),
        out_specs=whole,
        compiler_params=pltpu.CompilerParams(vmem_limit_bytes=LIMIT),
        cost_estimate=pl.CostEstimate(flops=0, bytes_accessed=4 * len(parts) * parts[0].size, transcendentals=0),
    )(*parts)


def columns_of(coupling_ref, place, core, rows):
    devices = lax.axis_size("occ")
    me = lax.axis_index("occ")
    me = me - lax.rem(me, CORES) + core
    start = pl.multiple_of(lax.rem(me - STEPS[place] + devices, devices) * rows, rows)
    return coupling_ref[:, pl.ds(start, rows)]


def near_kernel(mask_ref, amps_ref, blocks_ref, coupling_ref, near_ref, total_ref, held, sem):
    load = pltpu.make_async_copy(blocks_ref.at[0, 2], held, sem)
    load.start()
    core = lax.rem(lax.axis_index("occ"), CORES)
    chips, rows = near_ref.shape[:2]
    total = jnp.zeros(total_ref.shape, jnp.float32)
    for chip in range(chips):
        total += jnp.dot(
            columns_of(coupling_ref, chip, core, rows), near_ref[chip], preferred_element_type=jnp.float32
        )
    load.wait()
    flag = mask_ref[0, 2].astype(jnp.float32)
    total_ref[...] = total + flag * jnp.dot(amps_ref[...], held[...], preferred_element_type=jnp.float32)


def near_terms(mask, amps, integrals, coupling, near):
    rows, tile = amps.shape
    whole = pl.BlockSpec(memory_space=pltpu.VMEM)
    return pl.pallas_call(
        near_kernel,
        out_shape=jax.ShapeDtypeStruct((rows, tile), jnp.float32),
        in_specs=[pl.BlockSpec(memory_space=pltpu.SMEM), whole, pl.BlockSpec(memory_space=pl.ANY), whole, whole],
        out_specs=whole,
        scratch_shapes=[pltpu.VMEM((tile, tile), amps.dtype), pltpu.SemaphoreType.DMA],
        compiler_params=pltpu.CompilerParams(vmem_limit_bytes=LIMIT),
        cost_estimate=pl.CostEstimate(
            flops=16 * coupling.size * tile, bytes_accessed=2 * (coupling.size + near.size), transcendentals=0
        ),
    )(mask, amps, integrals, coupling, near)


def far_kernel(coupling_ref, far_ref, total_ref, sum_ref):
    core = CORES - 1 - lax.rem(lax.axis_index("occ"), CORES)
    chips, rows = far_ref.shape[:2]
    total = total_ref[...]
    for chip in range(chips):
        total += jnp.dot(
            columns_of(coupling_ref, chip, core, rows), far_ref[chip], preferred_element_type=jnp.float32
        )
    sum_ref[...] = total


def far_terms(coupling, far, total):
    whole = pl.BlockSpec(memory_space=pltpu.VMEM)
    return pl.pallas_call(
        far_kernel,
        out_shape=jax.ShapeDtypeStruct(total.shape, jnp.float32),
        in_specs=[whole] * 3,
        out_specs=whole,
        compiler_params=pltpu.CompilerParams(vmem_limit_bytes=LIMIT),
        cost_estimate=pl.CostEstimate(
            flops=coupling.size * total.shape[1], bytes_accessed=2 * (coupling.size + far.size), transcendentals=0
        ),
    )(coupling, far, total)


def body(amps, integrals, mask, pair_coupling, occ_energy, vir_energy):
    devices = lax.axis_size("occ")
    rows = [amps] + [
        lax.ppermute(amps, "occ", [(i, (i + step) % devices) for i in range(devices)]) for step in STEPS[1:]
    ]
    products = terms(mask, amps, integrals)
    arrived = [
        shifted(products[i].astype(jnp.float16), "vir", (1, 2, -1, -2)[i]) for i in (3, 2, 1, 0)
    ]
    near = joined(rows)
    far = lax.ppermute(near, "occ", [(i, i ^ 1) for i in range(devices)])
    total = near_terms(mask, amps, integrals, pair_coupling, near)
    total = far_terms(pair_coupling, far, total)
    total = total + sum(a.astype(jnp.float32) for a in arrived) * (1.0 / SCALE)
    return total / (occ_energy[:, None] - vir_energy[None, :])


def solution(mesh):
    placed = (
        P("occ", "vir"),
        P("vir", None, None, None),
        P("vir", None),
        P("occ", None),
        P("occ"),
        P("vir"),
    )
    return jax.shard_map(
        body, mesh=mesh, in_specs=placed, out_specs=P("occ", "vir"), check_vma=False
    )
```

```python
import jax
import jax.numpy as jnp
from jax import lax
from jax.experimental import pallas as pl
from jax.experimental.pallas import tpu as pltpu
from jax.sharding import PartitionSpec as P

SCALE = 64.0
SENT = (1, 0, 3, 4)
LIMIT = 52 * 2**20


def shifted(block, axis, distance):
    devices = range(lax.axis_size(axis))
    route = [(i - distance, i) for i in devices if i - distance in devices]
    return lax.ppermute(block, axis, route)


def terms_kernel(mask_ref, amps_ref, blocks_ref, wide_ref, *rest):
    out_refs, (held, in_sems, out_sems) = rest[:4], rest[4:]
    loads = [
        pltpu.make_async_copy(blocks_ref.at[0, k], held.at[i], in_sems.at[i])
        for i, k in enumerate(SENT)
    ]
    copies = [
        pltpu.make_async_copy(amps_ref, wide_ref.at[i], out_sems.at[i])
        for i in range(wide_ref.shape[0])
    ]
    for load in loads:
        load.start()
    for copy in copies:
        copy.start()
    for i, k in enumerate(SENT):
        loads[i].wait()
        flag = mask_ref[0, k].astype(jnp.float32) * SCALE
        out_refs[i][...] = flag * jnp.dot(
            amps_ref[...], held[i], preferred_element_type=jnp.float32
        )
    for copy in copies:
        copy.wait()


def terms(mask, amps, integrals, chips):
    rows, tile = amps.shape
    whole = pl.BlockSpec(memory_space=pltpu.VMEM)
    product = jax.ShapeDtypeStruct((rows, tile), jnp.float32)
    return pl.pallas_call(
        terms_kernel,
        out_shape=(jax.ShapeDtypeStruct((chips, rows, tile), amps.dtype), *(product,) * 4),
        in_specs=[pl.BlockSpec(memory_space=pltpu.SMEM), whole, pl.BlockSpec(memory_space=pl.ANY)],
        out_specs=(pl.BlockSpec(memory_space=pl.ANY), *(whole,) * 4),
        scratch_shapes=[
            pltpu.VMEM((4, tile, tile), amps.dtype),
            pltpu.SemaphoreType.DMA((4,)),
            pltpu.SemaphoreType.DMA((chips,)),
        ],
        compiler_params=pltpu.CompilerParams(vmem_limit_bytes=LIMIT),
        cost_estimate=pl.CostEstimate(
            flops=8 * rows * tile * tile, bytes_accessed=8 * tile * tile, transcendentals=0
        ),
    )(mask, amps, integrals)


def rest_kernel(mask_ref, amps_ref, blocks_ref, coupling_ref, rows_ref, total_ref, own, held, sems):
    parts, rows = rows_ref.shape[:2]
    load = pltpu.make_async_copy(blocks_ref.at[0, 2], own, sems.at[parts])
    loads = [pltpu.make_async_copy(rows_ref.at[i], held.at[i], sems.at[i]) for i in range(parts)]
    load.start()
    for part in loads:
        part.start()
    load.wait()
    flag = mask_ref[0, 2].astype(jnp.float32)
    total = flag * jnp.dot(amps_ref[...], own[...], preferred_element_type=jnp.float32)
    for i in range(parts):
        loads[i].wait()
        total += jnp.dot(
            coupling_ref[:, i * rows : (i + 1) * rows], held[i], preferred_element_type=jnp.float32
        )
    total_ref[...] = total


def rest_of(mask, amps, integrals, coupling, gathered):
    rows, tile = amps.shape
    whole, there = pl.BlockSpec(memory_space=pltpu.VMEM), pl.BlockSpec(memory_space=pl.ANY)
    return pl.pallas_call(
        rest_kernel,
        out_shape=jax.ShapeDtypeStruct((rows, tile), jnp.float32),
        in_specs=[pl.BlockSpec(memory_space=pltpu.SMEM), whole, there, whole, there],
        out_specs=whole,
        scratch_shapes=[
            pltpu.VMEM((tile, tile), amps.dtype),
            pltpu.VMEM(gathered.shape, amps.dtype),
            pltpu.SemaphoreType.DMA((gathered.shape[0] + 1,)),
        ],
        compiler_params=pltpu.CompilerParams(vmem_limit_bytes=LIMIT),
        cost_estimate=pl.CostEstimate(
            flops=2 * (coupling.size + amps.size) * tile,
            bytes_accessed=2 * (coupling.size + gathered.size),
            transcendentals=0,
        ),
    )(mask, amps, integrals, coupling, gathered)


def body(amps, integrals, mask, pair_coupling, occ_energy, vir_energy):
    wide, *products = terms(mask, amps, integrals, lax.axis_size("occ"))
    gathered = lax.all_to_all(wide, "occ", 0, 0)
    arrived = [
        shifted(products[i].astype(jnp.float16), "vir", (1, 2, -1, -2)[i]) for i in (3, 2, 1, 0)
    ]
    total = rest_of(mask, amps, integrals, pair_coupling, gathered)
    total = total + sum(a.astype(jnp.float32) for a in arrived) * (1.0 / SCALE)
    return total / (occ_energy[:, None] - vir_energy[None, :])


def solution(mesh):
    placed = (
        P("occ", "vir"),
        P("vir", None, None, None),
        P("vir", None),
        P("occ", None),
        P("occ"),
        P("vir"),
    )
    return jax.shard_map(
        body, mesh=mesh, in_specs=placed, out_specs=P("occ", "vir"), check_vma=False
    )
```

```python
import jax
import jax.numpy as jnp
from jax import lax
from jax.experimental import pallas as pl
from jax.experimental.pallas import tpu as pltpu
from jax.sharding import PartitionSpec as P

SCALE = 64.0
OWN = 2
ORDER = (0, 4, 1, 3, OWN)
LIMIT = 51 * 2**20


def shifted(block, axis, distance):
    devices = range(lax.axis_size(axis))
    route = [(i - distance, i) for i in devices if i - distance in devices]
    return lax.ppermute(block, axis, route)


def repeat_kernel(amps_ref, wide_ref, sems):
    copies = [
        pltpu.make_async_copy(amps_ref, wide_ref.at[i], sems.at[i])
        for i in range(wide_ref.shape[0])
    ]
    for copy in copies:
        copy.start()
    for copy in copies:
        copy.wait()


def repeated(amps, times):
    there = pl.BlockSpec(memory_space=pl.ANY)
    return pl.pallas_call(
        repeat_kernel,
        out_shape=jax.ShapeDtypeStruct((times, *amps.shape), amps.dtype),
        in_specs=[there],
        out_specs=there,
        scratch_shapes=[pltpu.SemaphoreType.DMA((times,))],
        compiler_params=pltpu.CompilerParams(vmem_limit_bytes=54 * 2**20),
        cost_estimate=pl.CostEstimate(flops=0, bytes_accessed=2 * times * amps.size, transcendentals=0),
    )(amps)


def terms_kernel(mask_ref, amps_ref, blocks_ref, *rest):
    out_refs, (held, sems) = rest[:5], rest[5:]
    loads = [
        pltpu.make_async_copy(blocks_ref.at[0, k], held.at[i], sems.at[i])
        for i, k in enumerate(ORDER)
    ]
    for load in loads:
        load.start()
    for i, k in enumerate(ORDER):
        loads[i].wait()
        flag = mask_ref[0, k].astype(jnp.float32) * (1.0 if k == OWN else SCALE)
        out_refs[i][...] = flag * jnp.dot(
            amps_ref[...], held[i], preferred_element_type=jnp.float32
        )


def terms(mask, amps, integrals):
    rows, tile = amps.shape
    whole = pl.BlockSpec(memory_space=pltpu.VMEM)
    return pl.pallas_call(
        terms_kernel,
        out_shape=(jax.ShapeDtypeStruct((rows, tile), jnp.float32),) * 5,
        in_specs=[pl.BlockSpec(memory_space=pltpu.SMEM), whole, pl.BlockSpec(memory_space=pl.ANY)],
        out_specs=(whole,) * 5,
        scratch_shapes=[pltpu.VMEM((5, tile, tile), amps.dtype), pltpu.SemaphoreType.DMA((5,))],
        compiler_params=pltpu.CompilerParams(vmem_limit_bytes=LIMIT),
        cost_estimate=pl.CostEstimate(
            flops=10 * rows * tile * tile, bytes_accessed=10 * tile * tile, transcendentals=0
        ),
    )(mask, amps, integrals)


def rest_kernel(coupling_ref, rows_ref, total_ref):
    parts, rows = rows_ref.shape[:2]
    total = jnp.zeros(total_ref.shape, jnp.float32)
    for i in range(parts):
        total += jnp.dot(
            coupling_ref[:, i * rows : (i + 1) * rows], rows_ref[i], preferred_element_type=jnp.float32
        )
    total_ref[...] = total


def rest_of(coupling, gathered):
    whole = pl.BlockSpec(memory_space=pltpu.VMEM)
    return pl.pallas_call(
        rest_kernel,
        out_shape=jax.ShapeDtypeStruct((coupling.shape[0], gathered.shape[2]), jnp.float32),
        in_specs=[whole, whole],
        out_specs=whole,
        compiler_params=pltpu.CompilerParams(vmem_limit_bytes=16 * 2**20),
        cost_estimate=pl.CostEstimate(
            flops=2 * coupling.size * gathered.shape[2],
            bytes_accessed=2 * (coupling.size + gathered.size),
            transcendentals=0,
        ),
    )(coupling, gathered)


def body(amps, integrals, mask, pair_coupling, occ_energy, vir_energy):
    gathered = lax.all_to_all(repeated(amps, lax.axis_size("occ")), "occ", 0, 0)
    *products, own = terms(mask, amps, integrals)
    arrived = [
        shifted(products[i].astype(jnp.float16), "vir", OWN - ORDER[i]) for i in (3, 2, 1, 0)
    ]
    total = rest_of(pair_coupling, gathered) + own
    total = total + sum(a.astype(jnp.float32) for a in arrived) * (1.0 / SCALE)
    return total / (occ_energy[:, None] - vir_energy[None, :])


def solution(mesh):
    placed = (
        P("occ", "vir"),
        P("vir", None, None, None),
        P("vir", None),
        P("occ", None),
        P("occ"),
        P("vir"),
    )
    return jax.shard_map(
        body, mesh=mesh, in_specs=placed, out_specs=P("occ", "vir"), check_vma=False
    )
```

```python
import jax
import jax.numpy as jnp
from jax import lax
from jax.experimental import pallas as pl
from jax.experimental.pallas import tpu as pltpu
from jax.sharding import PartitionSpec as P

SCALE = 64.0
OWN = 2
ORDER = (0, 4, 1, 3, OWN)
LIMIT = 50 * 2**20


def shifted(block, axis, distance):
    devices = range(lax.axis_size(axis))
    route = [(i - distance, i) for i in devices if i - distance in devices]
    return lax.ppermute(block, axis, route)


def repeat_kernel(amps_ref, wide_ref, held, sems):
    times = wide_ref.shape[0]
    load = pltpu.make_async_copy(amps_ref, held, sems.at[times])
    load.start()
    load.wait()
    copies = [pltpu.make_async_copy(held, wide_ref.at[i], sems.at[i]) for i in range(times)]
    for copy in copies:
        copy.start()
    for copy in copies:
        copy.wait()


def repeated(amps, times):
    there = pl.BlockSpec(memory_space=pl.ANY)
    return pl.pallas_call(
        repeat_kernel,
        out_shape=jax.ShapeDtypeStruct((times, *amps.shape), amps.dtype),
        in_specs=[there],
        out_specs=there,
        scratch_shapes=[pltpu.VMEM(amps.shape, amps.dtype), pltpu.SemaphoreType.DMA((times + 1,))],
        compiler_params=pltpu.CompilerParams(vmem_limit_bytes=54 * 2**20),
        cost_estimate=pl.CostEstimate(flops=0, bytes_accessed=2 * times * amps.size, transcendentals=0),
    )(amps)


def terms_kernel(mask_ref, amps_ref, blocks_ref, *rest):
    out_refs, (held, sems) = rest[:5], rest[5:]
    loads = [
        pltpu.make_async_copy(blocks_ref.at[0, k], held.at[i], sems.at[i])
        for i, k in enumerate(ORDER)
    ]
    for load in loads:
        load.start()
    for i, k in enumerate(ORDER):
        loads[i].wait()
        flag = mask_ref[0, k].astype(jnp.float32) * (1.0 if k == OWN else SCALE)
        out_refs[i][...] = flag * jnp.dot(
            amps_ref[...], held[i], preferred_element_type=jnp.float32
        )


def terms(mask, amps, integrals):
    rows, tile = amps.shape
    whole = pl.BlockSpec(memory_space=pltpu.VMEM)
    return pl.pallas_call(
        terms_kernel,
        out_shape=(jax.ShapeDtypeStruct((rows, tile), jnp.float32),) * 5,
        in_specs=[pl.BlockSpec(memory_space=pltpu.SMEM), whole, pl.BlockSpec(memory_space=pl.ANY)],
        out_specs=(whole,) * 5,
        scratch_shapes=[pltpu.VMEM((5, tile, tile), amps.dtype), pltpu.SemaphoreType.DMA((5,))],
        compiler_params=pltpu.CompilerParams(vmem_limit_bytes=LIMIT),
        cost_estimate=pl.CostEstimate(
            flops=10 * rows * tile * tile, bytes_accessed=10 * tile * tile, transcendentals=0
        ),
    )(mask, amps, integrals)


def rest_kernel(coupling_ref, rows_ref, total_ref, held, sems):
    parts, rows = rows_ref.shape[:2]
    loads = [pltpu.make_async_copy(rows_ref.at[i], held.at[i], sems.at[i]) for i in range(parts)]
    for part in loads:
        part.start()
    total = jnp.zeros(total_ref.shape, jnp.float32)
    for i in range(parts):
        loads[i].wait()
        total += jnp.dot(
            coupling_ref[:, i * rows : (i + 1) * rows], held[i], preferred_element_type=jnp.float32
        )
    total_ref[...] = total


def rest_of(coupling, gathered):
    whole, there = pl.BlockSpec(memory_space=pltpu.VMEM), pl.BlockSpec(memory_space=pl.ANY)
    return pl.pallas_call(
        rest_kernel,
        out_shape=jax.ShapeDtypeStruct((coupling.shape[0], gathered.shape[2]), jnp.float32),
        in_specs=[whole, there],
        out_specs=whole,
        scratch_shapes=[
            pltpu.VMEM(gathered.shape, gathered.dtype),
            pltpu.SemaphoreType.DMA((gathered.shape[0],)),
        ],
        compiler_params=pltpu.CompilerParams(vmem_limit_bytes=52 * 2**20),
        cost_estimate=pl.CostEstimate(
            flops=2 * coupling.size * gathered.shape[2],
            bytes_accessed=2 * (coupling.size + gathered.size),
            transcendentals=0,
        ),
    )(coupling, gathered)


def body(amps, integrals, mask, pair_coupling, occ_energy, vir_energy):
    gathered = lax.all_to_all(repeated(amps, lax.axis_size("occ")), "occ", 0, 0)
    *products, own = terms(mask, amps, integrals)
    arrived = [
        shifted(products[i].astype(jnp.float16), "vir", OWN - ORDER[i]) for i in (3, 2, 1, 0)
    ]
    total = rest_of(pair_coupling, gathered) + own
    total = total + sum(a.astype(jnp.float32) for a in arrived) * (1.0 / SCALE)
    return total / (occ_energy[:, None] - vir_energy[None, :])


def solution(mesh):
    placed = (
        P("occ", "vir"),
        P("vir", None, None, None),
        P("vir", None),
        P("occ", None),
        P("occ"),
        P("vir"),
    )
    return jax.shard_map(
        body, mesh=mesh, in_specs=placed, out_specs=P("occ", "vir"), check_vma=False
    )
```

```python
import functools

import jax
import jax.numpy as jnp
from jax import lax
from jax.experimental import pallas as pl
from jax.experimental.pallas import tpu as pltpu
from jax.sharding import PartitionSpec as P

SCALE = 64.0
OWN = 2
ORDER = (0, 4, 1, 3, OWN)
LIMIT = 48 * 2**20
HALF_LIMIT = 8 * 2**20
CORES = 2
NEAR_WORK = 64


def shifted(block, axis, distance):
    devices = range(lax.axis_size(axis))
    route = [(i - distance, i) for i in devices if i - distance in devices]
    return lax.ppermute(block, axis, route)


def repeat_kernel(amps_ref, wide_ref, held, sems):
    times = wide_ref.shape[0]
    load = pltpu.make_async_copy(amps_ref, held, sems.at[times])
    load.start()
    load.wait()
    copies = [pltpu.make_async_copy(held, wide_ref.at[i], sems.at[i]) for i in range(times)]
    for copy in copies:
        copy.start()
    for copy in copies:
        copy.wait()


def repeated(amps, times):
    there = pl.BlockSpec(memory_space=pl.ANY)
    return pl.pallas_call(
        repeat_kernel,
        out_shape=jax.ShapeDtypeStruct((times, *amps.shape), amps.dtype),
        in_specs=[there],
        out_specs=there,
        scratch_shapes=[pltpu.VMEM(amps.shape, amps.dtype), pltpu.SemaphoreType.DMA((times + 1,))],
        compiler_params=pltpu.CompilerParams(vmem_limit_bytes=54 * 2**20),
        cost_estimate=pl.CostEstimate(flops=0, bytes_accessed=2 * times * amps.size, transcendentals=0),
    )(amps)


def terms_kernel(mask_ref, amps_ref, blocks_ref, *rest):
    out_refs, (held, sems) = rest[:5], rest[5:]
    loads = [
        pltpu.make_async_copy(blocks_ref.at[0, k], held.at[i], sems.at[i])
        for i, k in enumerate(ORDER)
    ]
    for load in loads:
        load.start()
    for i, k in enumerate(ORDER):
        loads[i].wait()
        flag = mask_ref[0, k].astype(jnp.float32) * (1.0 if k == OWN else SCALE)
        out_refs[i][...] = flag * jnp.dot(
            amps_ref[...], held[i], preferred_element_type=jnp.float32
        )


def terms(mask, amps, integrals):
    rows, tile = amps.shape
    whole = pl.BlockSpec(memory_space=pltpu.VMEM)
    return pl.pallas_call(
        terms_kernel,
        out_shape=(jax.ShapeDtypeStruct((rows, tile), jnp.float32),) * 5,
        in_specs=[pl.BlockSpec(memory_space=pltpu.SMEM), whole, pl.BlockSpec(memory_space=pl.ANY)],
        out_specs=(whole,) * 5,
        scratch_shapes=[pltpu.VMEM((5, tile, tile), amps.dtype), pltpu.SemaphoreType.DMA((5,))],
        compiler_params=pltpu.CompilerParams(vmem_limit_bytes=LIMIT),
        cost_estimate=pl.CostEstimate(
            flops=10 * rows * tile * tile, bytes_accessed=10 * tile * tile, transcendentals=0
        ),
    )(mask, amps, integrals)


def columns_of(coupling_ref, chip, core, rows):
    start = pl.multiple_of((CORES * chip + core) * rows, rows)
    return coupling_ref[:, pl.ds(start, rows)]


def half_kernel(flip, coupling_ref, rows_ref, before_ref, total_ref):
    core = lax.axis_index("core")
    core = CORES - 1 - core if flip else core
    chips, rows = rows_ref.shape[:2]
    total = before_ref[...]
    for chip in range(chips):
        total += jnp.dot(
            columns_of(coupling_ref, chip, core, rows), rows_ref[chip], preferred_element_type=jnp.float32
        )
    total_ref[...] = total


def half_of(coupling, gathered, before, flip, flops):
    whole = pl.BlockSpec(memory_space=pltpu.VMEM)
    return pl.pallas_call(
        functools.partial(half_kernel, flip),
        out_shape=jax.ShapeDtypeStruct(before.shape, jnp.float32),
        in_specs=[whole] * 3,
        out_specs=whole,
        compiler_params=pltpu.CompilerParams(vmem_limit_bytes=HALF_LIMIT),
        cost_estimate=pl.CostEstimate(
            flops=flops, bytes_accessed=2 * (coupling.size + gathered.size), transcendentals=0
        ),
    )(coupling, gathered, before)


def body(amps, integrals, mask, pair_coupling, occ_energy, vir_energy):
    near = lax.all_to_all(repeated(amps, lax.axis_size("x")), "x", 0, 0)
    *products, own = terms(mask, amps, integrals)
    arrived = [
        shifted(products[i].astype(jnp.float16), "vir", OWN - ORDER[i]) for i in (0, 1, 2, 3)
    ]
    far = lax.ppermute(near, "core", [(i, CORES - 1 - i) for i in range(CORES)])
    work = pair_coupling.size * amps.shape[1]
    total = half_of(pair_coupling, near, own, False, NEAR_WORK * work)
    total = half_of(pair_coupling, far, total, True, work)
    total = total + sum(a.astype(jnp.float32) for a in arrived) * (1.0 / SCALE)
    return total / (occ_energy[:, None] - vir_energy[None, :])


def solution(mesh):
    devices = mesh.devices.reshape(-1, CORES, mesh.shape["vir"])
    lines = jax.sharding.Mesh(devices, ("x", "core", "vir"))
    occ = ("x", "core")
    placed = (
        P(occ, "vir"),
        P("vir", None, None, None),
        P("vir", None),
        P(occ, None),
        P(occ),
        P("vir"),
    )
    return jax.shard_map(
        body, mesh=lines, in_specs=placed, out_specs=P(occ, "vir"), check_vma=False
    )
```

```python
import functools

import jax
import jax.numpy as jnp
from jax import lax
from jax.experimental import pallas as pl
from jax.experimental.pallas import tpu as pltpu
from jax.sharding import PartitionSpec as P

SCALE = 64.0
OWN = 2
ORDER = (0, 4, 1, 3, OWN)
LIMIT = 48 * 2**20
HALF_LIMIT = 8 * 2**20
CORES = 2
NEAR_WORK = 64


def shifted(block, axis, distance):
    devices = range(lax.axis_size(axis))
    route = [(i - distance, i) for i in devices if i - distance in devices]
    return lax.ppermute(block, axis, route)


def terms_kernel(mask_ref, amps_ref, blocks_ref, *rest):
    out_refs, (held, sems) = rest[:5], rest[5:]
    loads = [
        pltpu.make_async_copy(blocks_ref.at[0, k], held.at[i], sems.at[i])
        for i, k in enumerate(ORDER)
    ]
    for load in loads:
        load.start()
    for i, k in enumerate(ORDER):
        loads[i].wait()
        flag = mask_ref[0, k].astype(jnp.float32) * (1.0 if k == OWN else SCALE)
        out_refs[i][...] = flag * jnp.dot(
            amps_ref[...], held[i], preferred_element_type=jnp.float32
        )


def terms(mask, amps, integrals):
    rows, tile = amps.shape
    whole = pl.BlockSpec(memory_space=pltpu.VMEM)
    return pl.pallas_call(
        terms_kernel,
        out_shape=(jax.ShapeDtypeStruct((rows, tile), jnp.float32),) * 5,
        in_specs=[pl.BlockSpec(memory_space=pltpu.SMEM), whole, pl.BlockSpec(memory_space=pl.ANY)],
        out_specs=(whole,) * 5,
        scratch_shapes=[pltpu.VMEM((5, tile, tile), amps.dtype), pltpu.SemaphoreType.DMA((5,))],
        compiler_params=pltpu.CompilerParams(vmem_limit_bytes=LIMIT),
        cost_estimate=pl.CostEstimate(
            flops=10 * rows * tile * tile, bytes_accessed=10 * tile * tile, transcendentals=0
        ),
    )(mask, amps, integrals)


def columns_of(coupling_ref, chip, core, rows):
    start = pl.multiple_of((CORES * chip + core) * rows, rows)
    return coupling_ref[:, pl.ds(start, rows)]


def half_kernel(flip, coupling_ref, rows_ref, before_ref, total_ref):
    core = lax.axis_index("core")
    core = CORES - 1 - core if flip else core
    chips, rows = rows_ref.shape[:2]
    total = before_ref[...]
    for chip in range(chips):
        total += jnp.dot(
            columns_of(coupling_ref, chip, core, rows), rows_ref[chip], preferred_element_type=jnp.float32
        )
    total_ref[...] = total


def half_of(coupling, gathered, before, flip, flops):
    whole = pl.BlockSpec(memory_space=pltpu.VMEM)
    return pl.pallas_call(
        functools.partial(half_kernel, flip),
        out_shape=jax.ShapeDtypeStruct(before.shape, jnp.float32),
        in_specs=[whole] * 3,
        out_specs=whole,
        compiler_params=pltpu.CompilerParams(vmem_limit_bytes=HALF_LIMIT),
        cost_estimate=pl.CostEstimate(
            flops=flops, bytes_accessed=2 * (coupling.size + gathered.size), transcendentals=0
        ),
    )(coupling, gathered, before)


def body(amps, integrals, mask, pair_coupling, occ_energy, vir_energy):
    wide = jnp.broadcast_to(amps[None], (lax.axis_size("x"), *amps.shape))
    near = lax.all_to_all(wide, "x", 0, 0)
    *products, own = terms(mask, amps, integrals)
    arrived = [
        shifted(products[i].astype(jnp.float16), "vir", OWN - ORDER[i]) for i in (0, 1, 2, 3)
    ]
    far = lax.ppermute(near, "core", [(i, CORES - 1 - i) for i in range(CORES)])
    work = pair_coupling.size * amps.shape[1]
    total = half_of(pair_coupling, near, own, False, NEAR_WORK * work)
    total = half_of(pair_coupling, far, total, True, work)
    total = total + sum(a.astype(jnp.float32) for a in arrived) * (1.0 / SCALE)
    return total / (occ_energy[:, None] - vir_energy[None, :])


def solution(mesh):
    devices = mesh.devices.reshape(-1, CORES, mesh.shape["vir"])
    lines = jax.sharding.Mesh(devices, ("x", "core", "vir"))
    occ = ("x", "core")
    placed = (
        P(occ, "vir"),
        P("vir", None, None, None),
        P("vir", None),
        P(occ, None),
        P(occ),
        P("vir"),
    )
    return jax.shard_map(
        body, mesh=lines, in_specs=placed, out_specs=P(occ, "vir"), check_vma=False
    )
```

```python
import functools

import jax
import jax.numpy as jnp
from jax import lax
from jax.experimental import pallas as pl
from jax.experimental.pallas import tpu as pltpu
from jax.sharding import PartitionSpec as P

SCALE = 64.0
OWN = 2
ORDER = (0, 4, 1, 3, OWN)
LIMIT = 16 * 2**20
HALF_LIMIT = 8 * 2**20
CORES = 2
NEAR_WORK = 64


def shifted(block, axis, distance):
    devices = range(lax.axis_size(axis))
    route = [(i - distance, i) for i in devices if i - distance in devices]
    return lax.ppermute(block, axis, route)


def terms_kernel(mask_ref, amps_ref, blocks_ref, *out_refs):
    for k, out_ref in zip(ORDER, out_refs):
        flag = mask_ref[0, k].astype(jnp.float32) * (1.0 if k == OWN else SCALE)
        out_ref[...] = flag * jnp.dot(
            amps_ref[...], blocks_ref[0, k], preferred_element_type=jnp.float32
        )


def terms(mask, amps, integrals):
    rows, tile = amps.shape
    whole = pl.BlockSpec(memory_space=pltpu.VMEM)
    return pl.pallas_call(
        terms_kernel,
        out_shape=(jax.ShapeDtypeStruct((rows, tile), jnp.float32),) * 5,
        in_specs=[pl.BlockSpec(memory_space=pltpu.SMEM), whole, whole],
        out_specs=(whole,) * 5,
        compiler_params=pltpu.CompilerParams(vmem_limit_bytes=LIMIT),
        cost_estimate=pl.CostEstimate(
            flops=10 * rows * tile * tile, bytes_accessed=10 * tile * tile, transcendentals=0
        ),
    )(mask, amps, integrals)


def columns_of(coupling_ref, chip, core, rows):
    start = pl.multiple_of((CORES * chip + core) * rows, rows)
    return coupling_ref[:, pl.ds(start, rows)]


def half_kernel(flip, coupling_ref, rows_ref, before_ref, total_ref):
    core = lax.axis_index("core")
    core = CORES - 1 - core if flip else core
    chips, rows = rows_ref.shape[:2]
    total = before_ref[...]
    for chip in range(chips):
        total += jnp.dot(
            columns_of(coupling_ref, chip, core, rows), rows_ref[chip], preferred_element_type=jnp.float32
        )
    total_ref[...] = total


def half_of(coupling, gathered, before, flip, flops):
    whole = pl.BlockSpec(memory_space=pltpu.VMEM)
    return pl.pallas_call(
        functools.partial(half_kernel, flip),
        out_shape=jax.ShapeDtypeStruct(before.shape, jnp.float32),
        in_specs=[whole] * 3,
        out_specs=whole,
        compiler_params=pltpu.CompilerParams(vmem_limit_bytes=HALF_LIMIT),
        cost_estimate=pl.CostEstimate(
            flops=flops, bytes_accessed=2 * (coupling.size + gathered.size), transcendentals=0
        ),
    )(coupling, gathered, before)


def body(amps, integrals, mask, pair_coupling, occ_energy, vir_energy):
    wide = jnp.broadcast_to(amps[None], (lax.axis_size("x"), *amps.shape))
    near = lax.all_to_all(wide, "x", 0, 0)
    *products, own = terms(mask, amps, integrals)
    arrived = [
        shifted(products[i].astype(jnp.float16), "vir", OWN - ORDER[i]) for i in (0, 1, 2, 3)
    ]
    far = lax.ppermute(near, "core", [(i, CORES - 1 - i) for i in range(CORES)])
    work = pair_coupling.size * amps.shape[1]
    total = half_of(pair_coupling, near, own, False, NEAR_WORK * work)
    total = half_of(pair_coupling, far, total, True, work)
    total = total + sum(a.astype(jnp.float32) for a in arrived) * (1.0 / SCALE)
    return total / (occ_energy[:, None] - vir_energy[None, :])


def solution(mesh):
    devices = mesh.devices.reshape(-1, CORES, mesh.shape["vir"])
    lines = jax.sharding.Mesh(devices, ("x", "core", "vir"))
    occ = ("x", "core")
    placed = (
        P(occ, "vir"),
        P("vir", None, None, None),
        P("vir", None),
        P(occ, None),
        P(occ),
        P("vir"),
    )
    return jax.shard_map(
        body, mesh=lines, in_specs=placed, out_specs=P(occ, "vir"), check_vma=False
    )
```
